32 devices in a mesh: graph: 8 (over z, x), rep: 4 (over y, core).
Axes of the slice: x: 2, y: 2, z: 4, core: 2. Of those that a mesh axis runs over, the one named last changes fastest.
Arguments:
- node_feats: bfloat16 [4, 128, 49, 256], P('rep', 'graph'), may hold values from -6 to 6
- species: int32 [4, 128], P('rep', 'graph'), may hold values from 0 to 89
- charge: int32 [4], P('rep'), may hold values from 0 to 8
- species_table: float32 [90, 256], replicated, may hold values from -6 to 6
- charge_table: float32 [9, 256], replicated, may hold values from -6 to 6
- so2_weight: bfloat16 [1792, 1792], replicated, may hold values from -0.125 to 0.125
- edge_frame: bfloat16 [4, 49, 2048], P('rep', None, 'graph'), as said below
- edge_src: int32 [4, 2048], P('rep', 'graph'), may hold values from 0 to 127, as said below
- edge_dst: int32 [4, 2048], P('rep', 'graph'), may hold values from 0 to 127, as said below
- edge_count: int32 [4, 8], P('rep', 'graph'), may hold values from 32 to 192, as said below
- out_cotangent: bfloat16 [4, 128, 49, 256], P('rep', 'graph'), may hold values from -6 to 6
Outputs:
- updated_feats: bfloat16 [4, 128, 49, 256], P('rep', 'graph')
- feat_grad: bfloat16 [4, 128, 49, 256], P('rep', 'graph')
- weight_grad: float32 [3211264], P(('graph', 'rep'))
- species_grad: float32 [90, 256], replicated
- charge_grad: float32 [9, 256], replicated
The draws below stay inside these ranges and needn't reach their ends.
Inputs may be any that keep to these rules, and one draw needn't show every extreme that they name: `edge_count`: live slots of one device per cell. Two devices whose graph indices differ by half the axis hold at most 256 live slots together; in every cell some device holds exactly 192. `edge_src`: in a live slot the source atom's device (index // 16) is at most 2 devices from the slot's device along graph, cyclically; a slot that is not live holds its device's first atom. `edge_dst`: each slot's destination atom belongs to the device that holds the slot; a slot that is not live holds its device's first atom. `edge_frame`: for every edge and degree l the 2l+1 entries of degree l have unit sum of squares; the degree-0 entry is 1.
All inputs are finite; a program needn't handle non-finite values.
Results may differ from the reference program's by a relative error of at most 0.0066.
Values may be sent and summed in bfloat16 or wider, within the bound.
A program may use at most 128 MiB of HBM per device.

```python
import jax
import jax.numpy as jnp
from jax import lax

CH = 256
LMAX = 6
DEGREES = 7
COEF = 49
FEAT = 1792
SPECIES = 90
CHARGES = 9
REACH = 2
ATOMS_DEV = 16
ECAP = 256
CELLS = 4
ATOMS = 128
EDGES = 2048


def edge_plan(key):
    graph_count = EDGES // ECAP
    pair_count = graph_count // 2
    subkeys = jax.random.split(jax.random.fold_in(key, 7), 8)
    centre = jax.random.randint(subkeys[0], (CELLS, 1), 0, pair_count)
    pair_ids = jnp.arange(pair_count, dtype=jnp.int32)[None, :]
    distance = jnp.abs(pair_ids - centre)
    distance = jnp.minimum(distance, pair_count - distance)
    near_load = jax.random.randint(subkeys[1], (CELLS, pair_count), 5 * ECAP // 8, 3 * ECAP // 4 + 1)
    far_load = jax.random.randint(subkeys[2], (CELLS, pair_count), ECAP // 4, ECAP // 2 + 1)
    heavy_load = jnp.where(distance <= 1, near_load, far_load)
    heavy_load = jnp.where(distance == 0, 3 * ECAP // 4, heavy_load)
    light_load = jax.random.randint(subkeys[3], (CELLS, pair_count), ECAP // 8, ECAP // 4 + 1)
    heavy_low = jax.random.randint(subkeys[4], (CELLS, pair_count), 0, 2)
    low_half = jnp.where(heavy_low == 1, heavy_load, light_load)
    high_half = jnp.where(heavy_low == 1, light_load, heavy_load)
    counts = jnp.concatenate([low_half, high_half], axis=1).astype(jnp.int32)
    grid_shape = (CELLS, graph_count, ECAP)
    is_live = jnp.arange(ECAP, dtype=jnp.int32)[None, None, :] < counts[:, :, None]
    owners = jnp.arange(graph_count, dtype=jnp.int32)[None, :, None]
    target_atom = jax.random.randint(subkeys[5], grid_shape, 0, ATOMS_DEV)
    reach_step = jax.random.randint(subkeys[6], grid_shape, -REACH, REACH + 1)
    source_atom = jax.random.randint(subkeys[7], grid_shape, 0, ATOMS_DEV)
    first_atom = owners * ATOMS_DEV
    targets = jnp.where(is_live, first_atom + target_atom, first_atom)
    sources = jnp.where(is_live, (owners + reach_step) % graph_count * ATOMS_DEV + source_atom, first_atom)
    return (counts, sources.reshape(CELLS, EDGES).astype(jnp.int32), targets.reshape(CELLS, EDGES).astype(jnp.int32))


def draw_edge_count(key, part):
    return edge_plan(key)[0]


def draw_edge_src(key, part):
    return edge_plan(key)[1]


def draw_edge_dst(key, part):
    return edge_plan(key)[2]


def draw_edge_frame(key, part):
    gaussian = jax.random.normal(key, (CELLS, COEF, EDGES), jnp.float32)
    pieces = [jnp.ones((CELLS, 1, EDGES), jnp.float32)]
    for degree in range(1, LMAX + 1):
        block_rows = gaussian[:, degree * degree:(degree + 1) * (degree + 1), :]
        norm_rows = jnp.sqrt(jnp.sum(block_rows * block_rows, axis=1, keepdims=True))
        pieces.append(block_rows / norm_rows)
    return jnp.concatenate(pieces, axis=1).astype(jnp.bfloat16)


def place_ends(drawn, stream_key, low, high):
    place = [jax.random.randint(jax.random.fold_in(stream_key, axis), (), 0, length) for axis, length in enumerate(drawn.shape)]
    main_axis = drawn.shape.index(max(drawn.shape))
    neighbour = place[:main_axis] + [(place[main_axis] + 1) % drawn.shape[main_axis]] + place[main_axis + 1:]
    return drawn.at[tuple(place)].set(low).at[tuple(neighbour)].set(high)


def level_of(rng, dims, cuts, low, top_value):
    loudness = 1.0
    for dim, shards_of in cuts:
        steps = jax.random.uniform(jax.random.fold_in(jax.random.fold_in(rng, 6), dim), (shards_of,), jnp.float32, low / len(cuts), top_value / len(cuts))
        loudness = loudness * jnp.repeat(jnp.exp(steps), dims[dim] // shards_of).reshape((-1,) + (1,) * (len(dims) - 1 - dim))
    return loudness


def centred(stream_key, dims, spread, bound, cuts=(), kind=jnp.bfloat16):
    gain = level_of(stream_key, dims, cuts, -0.22, 0.18) if cuts else 1.0
    entries = jax.random.normal(stream_key, dims, jnp.float32) * spread * gain
    return jnp.minimum(jnp.maximum(entries, -bound), bound).astype(kind)


def setup_inputs(seed: int = 0) -> dict:
    seeds = jax.random.split(jax.random.key(seed), 12)
    node_feats = centred(seeds[0], (CELLS, ATOMS, COEF, CH), 1.0, 6.0, ((0, 4), (1, 8)))
    species = place_ends(jax.random.randint(seeds[1], (CELLS, ATOMS), 0, SPECIES), jax.random.fold_in(seeds[1], 1), 0, SPECIES - 1).astype(jnp.int32)
    charge = place_ends(jax.random.randint(seeds[2], (CELLS,), 0, CHARGES), jax.random.fold_in(seeds[2], 1), 0, CHARGES - 1).astype(jnp.int32)
    species_table = centred(seeds[3], (SPECIES, CH), 1.0, 6.0, (), jnp.float32)
    charge_table = centred(seeds[4], (CHARGES, CH), 1.0, 6.0, (), jnp.float32)
    so2_weight = centred(seeds[5], (FEAT, FEAT), FEAT ** -0.5, 0.125)
    edge_frame = draw_edge_frame(jax.random.fold_in(seeds[11], 71), 0)
    edge_src = draw_edge_src(jax.random.fold_in(seeds[11], 71), 0)
    edge_dst = draw_edge_dst(jax.random.fold_in(seeds[11], 71), 0)
    edge_count = draw_edge_count(jax.random.fold_in(seeds[11], 71), 0)
    out_cotangent = centred(seeds[10], (CELLS, ATOMS, COEF, CH), 1.0, 6.0, ((0, 4), (1, 8)))
    return {"node_feats": node_feats, "species": species, "charge": charge, "species_table": species_table, "charge_table": charge_table, "so2_weight": so2_weight, "edge_frame": edge_frame, "edge_src": edge_src, "edge_dst": edge_dst, "edge_count": edge_count, "out_cotangent": out_cotangent}


MSG_SCALE = 0.25
PRECISE = lax.Precision.HIGHEST


def degree_spans():
    return [(degree * degree, (degree + 1) * (degree + 1)) for degree in range(LMAX + 1)]


def rotate_in(frame_rows, node_rows):
    pieces = [jnp.einsum("ke,ekc->ec", frame_rows[lower_k:upper_k], node_rows[:, lower_k:upper_k, :], precision=PRECISE) for lower_k, upper_k in degree_spans()]
    return jnp.stack(pieces, axis=1)


def rotate_out(frame_rows, edge_vals):
    pieces = [jnp.transpose(frame_rows[lower_k:upper_k])[:, :, None] * edge_vals[:, degree, :][:, None, :] for degree, (lower_k, upper_k) in enumerate(degree_spans())]
    return jnp.concatenate(pieces, axis=1)


def gate_forward(pre_act):
    return pre_act * jax.nn.sigmoid(pre_act[:, :1, :])


def gate_backward(pre_act, grad_out):
    sig_gate = jax.nn.sigmoid(pre_act[:, :1, :])
    cross_term = jnp.sum(grad_out * pre_act, axis=1, keepdims=True) * sig_gate * (1.0 - sig_gate)
    scaled = grad_out * sig_gate
    return jnp.concatenate([scaled[:, :1, :] + cross_term, scaled[:, 1:, :]], axis=1)


def round_trip(tensor):
    return lax.optimization_barrier(tensor.astype(jnp.bfloat16)).astype(jnp.float32)


def cell_pass(node_feats, species, charge, species_table, charge_table, so2_weight, edge_frame, edge_src, edge_dst, edge_count, out_cotangent):
    graph_count = EDGES // ECAP
    spec_hot = (species[:, None] == jnp.arange(SPECIES, dtype=jnp.int32)[None, :]).astype(jnp.float32)
    embedding = jnp.dot(spec_hot, species_table, precision=PRECISE) + charge_table[charge][None, :]
    features = node_feats.astype(jnp.float32)
    hidden = jnp.concatenate([features[:, :1, :] + embedding[:, None, :], features[:, 1:, :]], axis=1).astype(jnp.bfloat16)
    frames = jnp.transpose(edge_frame.astype(jnp.float32).reshape(COEF, graph_count, ECAP), (1, 0, 2))
    sources = edge_src.reshape(graph_count, ECAP)
    targets = edge_dst.reshape(graph_count, ECAP)
    owners = jnp.arange(graph_count, dtype=jnp.int32)
    slot_ids = jnp.arange(ECAP, dtype=jnp.int32)

    def edge_rows(frame_rows, source_ids, live_count):
        live_mask = (slot_ids < live_count).astype(jnp.float32)[:, None, None]
        rotated = rotate_in(frame_rows, hidden[source_ids].astype(jnp.float32)) * live_mask
        rotated = rotated.astype(jnp.bfloat16).reshape(ECAP, FEAT)
        pre_act = jnp.dot(rotated, so2_weight, preferred_element_type=jnp.float32).reshape(ECAP, DEGREES, CH)
        return live_mask, rotated, pre_act

    def forward_block(inputs):
        frame_rows, source_ids, target_ids, live_count, owner_id = inputs
        live_mask, rotated, pre_act = edge_rows(frame_rows, source_ids, live_count)
        gated = round_trip(gate_forward(pre_act))
        message = rotate_out(frame_rows, gated) * live_mask
        local_ids = (target_ids - owner_id * ATOMS_DEV).astype(jnp.int32)
        return jnp.zeros((ATOMS_DEV, COEF, CH), jnp.float32).at[local_ids].add(message)

    gathered = lax.map(forward_block, (frames, sources, targets, edge_count, owners))
    aggregate = gathered.reshape(ATOMS, COEF, CH)
    updated = (features + MSG_SCALE * aggregate).astype(jnp.bfloat16)
    cotangent = out_cotangent.astype(jnp.float32)

    def backward_block(carry, inputs):
        weight_sum, node_grad = carry
        frame_rows, source_ids, target_ids, live_count = inputs
        live_mask, rotated, pre_act = edge_rows(frame_rows, source_ids, live_count)
        grad_values = MSG_SCALE * rotate_in(frame_rows, cotangent[target_ids]) * live_mask
        grad_pre = gate_backward(pre_act, grad_values).astype(jnp.bfloat16).reshape(ECAP, FEAT)
        weight_sum = weight_sum + jnp.dot(jnp.transpose(rotated), grad_pre, preferred_element_type=jnp.float32)
        grad_rot = jnp.dot(grad_pre, jnp.transpose(so2_weight), preferred_element_type=jnp.float32)
        grad_rot = round_trip(grad_rot).reshape(ECAP, DEGREES, CH)
        back_rows = rotate_out(frame_rows, grad_rot) * live_mask
        partial_grad = jnp.zeros((ATOMS, COEF, CH), jnp.float32).at[source_ids].add(back_rows)
        node_grad = node_grad + round_trip(partial_grad)
        return (weight_sum, node_grad), None

    start_carry = (jnp.zeros((FEAT, FEAT), jnp.float32), jnp.zeros((ATOMS, COEF, CH), jnp.float32))
    (weight_sum, node_grad), _ = lax.scan(backward_block, start_carry, (frames, sources, targets, edge_count))
    feat_grad = (cotangent + node_grad).astype(jnp.bfloat16)
    invariant = node_grad[:, 0, :]
    species_grad = jnp.dot(jnp.transpose(spec_hot), invariant, precision=PRECISE)
    charge_hot = (jnp.arange(CHARGES, dtype=jnp.int32) == charge).astype(jnp.float32)
    charge_grad = charge_hot[:, None] * jnp.sum(invariant, axis=0)[None, :]
    return updated, feat_grad, weight_sum, species_grad, charge_grad


def reference(node_feats, species, charge, species_table, charge_table, so2_weight, edge_frame, edge_src, edge_dst, edge_count, out_cotangent):
    outcomes = [cell_pass(node_feats[cell_index], species[cell_index], charge[cell_index], species_table, charge_table, so2_weight, edge_frame[cell_index], edge_src[cell_index], edge_dst[cell_index], edge_count[cell_index], out_cotangent[cell_index]) for cell_index in range(CELLS)]
    updated = jnp.stack([outcome[0] for outcome in outcomes], axis=0)
    feat_grad = jnp.stack([outcome[1] for outcome in outcomes], axis=0)
    weight_grad = outcomes[0][2]
    species_grad = outcomes[0][3]
    charge_grad = outcomes[0][4]
    for outcome in outcomes[1:]:
        weight_grad = weight_grad + outcome[2]
        species_grad = species_grad + outcome[3]
        charge_grad = charge_grad + outcome[4]
    return updated, feat_grad, weight_grad.reshape(-1), species_grad, charge_grad
```

```python
import functools

import jax
import jax.numpy as jnp
from jax import lax
from jax.experimental import pallas as pl
from jax.experimental.pallas import tpu as pltpu
from jax.sharding import PartitionSpec as P

LMAX = 6
SPECIES = 90
CHARGES = 9
REACH = 2
NEAR = 2 * REACH + 1
MSG_SCALE = 0.25
PRECISE = lax.Precision.HIGHEST
MESH = pl.DeviceIdType.MESH
HOTS = 104
F32 = jnp.float32
BF16 = jnp.bfloat16
MIB = 1 << 20

OFFSETS = (-2, 2, -1, 1)


def degree_spans():
    return [(degree * degree, (degree + 1) * (degree + 1)) for degree in range(LMAX + 1)]


def dot_tn(left, right):
    return lax.dot_general(left, right, (((0,), (0,)), ((), ())), preferred_element_type=F32)


def dot_nn(left, right):
    return jnp.dot(left, right, preferred_element_type=F32)


def dot_nt(left, right):
    return lax.dot_general(left, right, (((1,), (1,)), ((), ())), preferred_element_type=F32)


def halo_kernel(size, feats_ref, spec_ref, charge_ref, stab_ref, ctab_ref, near_ref, hid, send_sem, recv_sem):
    atoms = feats_ref.shape[1]
    me = lax.axis_index("graph")
    rep = lax.axis_index("rep")
    barrier = pltpu.get_barrier_semaphore()
    for off in OFFSETS:
        pl.semaphore_signal(barrier, inc=1, device_id=(lax.rem(me + off + size, size), rep), device_id_type=MESH)
    spec_hot = (spec_ref[...] == lax.broadcasted_iota(jnp.int32, (atoms, SPECIES), 1)).astype(F32)
    charge_hot = (charge_ref[...] == lax.broadcasted_iota(jnp.int32, (atoms, CHARGES), 1)).astype(F32)
    embedding = jnp.dot(spec_hot, stab_ref[...], precision=PRECISE, preferred_element_type=F32) + jnp.dot(
        charge_hot, ctab_ref[...], precision=PRECISE, preferred_element_type=F32
    )
    hid[...] = feats_ref[...]
    hid[0] = (feats_ref[0].astype(F32) + embedding).astype(BF16)
    pl.semaphore_wait(barrier, len(OFFSETS))
    copies = []
    for i, off in enumerate(OFFSETS):
        slot = REACH - off
        copy = pltpu.make_async_remote_copy(
            src_ref=hid,
            dst_ref=near_ref.at[:, pl.ds(slot * atoms, atoms), :],
            send_sem=send_sem.at[i],
            recv_sem=recv_sem.at[i],
            device_id=(lax.rem(me + off + size, size), rep),
            device_id_type=MESH,
        )
        copy.start()
        copies.append(copy)
    near_ref[:, pl.ds(REACH * atoms, atoms), :] = hid[...]
    for copy in copies:
        copy.wait()


def compute_kernel(
    group_rows, pos_ref, near_ref, feats_ref, cot_ref, frame_ref, src_ref, dst_ref, w_ref,
    upd_ref, terms_ref, wp_ref, s_ref, d_ref, rot_ref, rott_ref, pre_ref, gv_ref, gp_ref, *rest,
):
    coef, near_atoms, ch = near_ref.shape
    atoms = feats_ref.shape[1]
    slots = src_ref.shape[1]
    me = pos_ref[0]
    live_count = pos_ref[1]
    size = pos_ref[2]
    live = lax.broadcasted_iota(jnp.int32, (1, slots), 1) < live_count
    sources = src_ref[...]
    rel = lax.rem(sources // atoms - me + REACH + size, size)
    local_src = jnp.where(live, rel * atoms + lax.rem(sources, atoms), -1)
    local_dst = jnp.where(live, dst_ref[...] - me * atoms, -1)
    s_hot = (lax.broadcasted_iota(jnp.int32, (near_atoms, slots), 0) == local_src).astype(F32)
    d_hot = (lax.broadcasted_iota(jnp.int32, (atoms, slots), 0) == local_dst).astype(F32)
    spans = degree_spans()
    for k in range(coef):
        row = frame_ref[pl.ds(k, 1), :]
        s_ref[k] = (s_hot * row).astype(BF16)
        d_ref[k] = (d_hot * row).astype(BF16)
    for l, (lo, hi) in enumerate(spans):
        cols = pl.ds(l * ch, ch)
        s_l = s_ref[lo:hi].reshape((hi - lo) * near_atoms, slots)
        rot = dot_tn(s_l, near_ref[lo:hi].reshape((hi - lo) * near_atoms, ch))
        rot_ref[:, cols] = rot.astype(BF16)
        rott_ref[cols, :] = jnp.transpose(rot).astype(BF16)
        d_l = d_ref[lo:hi].reshape((hi - lo) * atoms, slots)
        gv_ref[:, cols] = MSG_SCALE * dot_tn(d_l, cot_ref[lo:hi].reshape((hi - lo) * atoms, ch))

    def pre_body(l, carry):
        cols = pl.ds(pl.multiple_of(l * ch, ch), ch)
        pre_ref[:, cols] = dot_nn(rot_ref[...], w_ref[:, cols])
        return carry

    lax.fori_loop(0, LMAX + 1, pre_body, 0)
    sig = jax.nn.sigmoid(pre_ref[:, 0:ch])
    cross = jnp.zeros_like(sig)
    for l, (lo, hi) in enumerate(spans):
        cols = pl.ds(l * ch, ch)
        pre = pre_ref[:, cols]
        grad = gv_ref[:, cols]
        cross = cross + grad * pre
        values = (pre * sig).astype(BF16)
        d_l = d_ref[lo:hi].reshape((hi - lo) * atoms, slots)
        agg = dot_nn(d_l, values).reshape(hi - lo, atoms, ch)
        upd_ref[lo:hi] = (feats_ref[lo:hi].astype(F32) + MSG_SCALE * agg).astype(BF16)
        if l > 0:
            gp_ref[:, cols] = (grad * sig).astype(BF16)
    gp_ref[:, 0:ch] = (gv_ref[:, 0:ch] * sig + cross * sig * (1.0 - sig)).astype(BF16)

    for l, (lo, hi) in enumerate(spans):
        grad_rot = dot_nt(gp_ref[...], w_ref[pl.ds(l * ch, ch), :]).astype(BF16)
        s_l = s_ref[lo:hi].reshape((hi - lo) * near_atoms, slots)
        terms_ref[lo:hi] = dot_nn(s_l, grad_rot).astype(BF16).reshape(hi - lo, near_atoms, ch)

    if group_rows is None:

        def weight_flat(j, carry):
            cols = pl.ds(pl.multiple_of(j * ch, ch), ch)
            wp_ref[:, cols] = dot_nn(rott_ref[...], gp_ref[:, cols])
            return carry

        lax.fori_loop(0, LMAX + 1, weight_flat, 0)
        return
    wide_ref = rest[0]

    def weight_body(j, carry):
        cols = pl.ds(pl.multiple_of(j * ch, ch), ch)
        wide_ref[:, cols] = dot_nn(rott_ref[...], gp_ref[:, cols])
        return carry

    lax.fori_loop(0, LMAX + 1, weight_body, 0)
    half = wide_ref.shape[1] // 2

    def group_body(i, carry):
        rows = wide_ref[pl.ds(pl.multiple_of(i * group_rows, 8), group_rows), :]
        wp_ref[i] = jnp.concatenate([rows[:, :half], rows[:, half:]], axis=0).astype(BF16)
        return carry

    lax.fori_loop(0, wp_ref.shape[0], group_body, 0)


def bit_reversed(value, bits):
    return int(format(value, "0" + str(bits) + "b")[::-1], 2) if bits else 0


def stage_order(bits):
    return sorted(range(1 << bits), key=lambda t: -bit_reversed(t, bits))


def reduce_kernel(
    size, reps, bits, terms_ref, cot_ref, wp_ref, spec_ref, charge_ref,
    feat_ref, wg_ref, emb_ref,
    sent, got, near_got, emb_sent, emb_got, s_sem, r_sem, hs_sem, hr_sem, es_sem, er_sem,
):
    atoms = cot_ref.shape[1]
    me = lax.axis_index("graph")
    rep = lax.axis_index("rep")
    mine = me * reps + rep
    bit = [lax.rem(mine // (1 << b), 2) for b in range(bits)]

    def flipped(rel):
        total = 0
        for b in range(bits):
            total = total + (1 << b) * ((1 - bit[b]) if (rel >> b) & 1 else bit[b])
        return total

    def partner(b):
        other = flipped(1 << b)
        return (other // reps, lax.rem(other, reps))

    near_ids = [(lax.rem(me + off + size, size), rep) for off in OFFSETS]
    barrier = pltpu.get_barrier_semaphore()
    for device in near_ids + [partner(b) for b in range(bits)]:
        pl.semaphore_signal(barrier, inc=1, device_id=device, device_id_type=MESH)
    pl.semaphore_wait(barrier, len(near_ids) + bits)

    halo = []
    for i, off in enumerate(OFFSETS):
        copy = pltpu.make_async_remote_copy(
            src_ref=terms_ref.at[:, pl.ds((off + REACH) * atoms, atoms), :],
            dst_ref=near_got.at[i],
            send_sem=hs_sem.at[i],
            recv_sem=hr_sem.at[i],
            device_id=near_ids[i],
            device_id_type=MESH,
        )
        halo.append(copy)
    base = [sum(1 << (bits - 1 - q) for q in range(stage)) for stage in range(bits + 1)]
    copies = {}

    def launch(stage, t, source):
        slot = base[stage] + t
        copy = pltpu.make_async_remote_copy(
            src_ref=source,
            dst_ref=got.at[slot],
            send_sem=s_sem.at[slot],
            recv_sem=r_sem.at[slot],
            device_id=partner(stage),
            device_id_type=MESH,
        )
        copy.start()
        copies[stage, t] = copy

    for t in stage_order(bits - 1):
        launch(0, t, wp_ref.at[flipped(2 * t + 1)])
    for copy in halo:
        copy.start()

    def summed(stage, rel):
        total = wp_ref[flipped(rel)].astype(F32)
        for q in range(stage):
            total = total + got[base[q] + (rel >> (q + 1))].astype(F32)
        return total

    for stage in range(1, bits):
        for t in stage_order(bits - 1 - stage):
            rel = (2 * t + 1) << stage
            slot = base[stage] + t
            for q in range(stage):
                copies[q, rel >> (q + 1)].wait_recv()
            sent[slot - base[1]] = summed(stage, rel).astype(BF16)
            launch(stage, t, sent.at[slot - base[1]])

    for copy in halo:
        copy.wait_recv()
    grad = terms_ref[:, pl.ds(REACH * atoms, atoms), :].astype(F32)
    for i in range(len(OFFSETS)):
        grad = grad + near_got[i].astype(F32)
    feat_ref[...] = (cot_ref[...].astype(F32) + grad).astype(BF16)
    inv = grad[0]
    row_ids = lax.broadcasted_iota(jnp.int32, (HOTS, atoms), 0)
    hot = ((row_ids == spec_ref[...]) | (row_ids == SPECIES + charge_ref[...])).astype(F32)
    emb_ref[...] = jnp.dot(hot, inv, precision=PRECISE, preferred_element_type=F32)
    emb = []
    for b in range(bits):
        emb_sent[b] = emb_ref[...]
        copy = pltpu.make_async_remote_copy(
            src_ref=emb_sent.at[b],
            dst_ref=emb_got.at[b],
            send_sem=es_sem.at[b],
            recv_sem=er_sem.at[b],
            device_id=partner(b),
            device_id_type=MESH,
        )
        copy.start()
        copy.wait_recv()
        emb_ref[...] = emb_ref[...] + emb_got[b]
        emb.append(copy)

    for q in range(bits):
        copies[q, 0].wait_recv()
    total = summed(bits, 0)
    rows = wg_ref.shape[0] // 14
    for j in range(14):
        lanes = (j % 7) * 128
        part = (j // 7) * rows
        wg_ref[pl.ds(j, rows, stride=14), :] = total[part : part + rows, lanes : lanes + 128]
    for copy in list(copies.values()) + halo + emb:
        copy.wait_send()


def vmem(count):
    return [pl.BlockSpec(memory_space=pltpu.VMEM)] * count


def local(
    size, reps, node_feats, species, charge, species_table, charge_table, so2_weight,
    edge_frame, edge_src, edge_dst, edge_count, out_cotangent,
):
    _, atoms, coef, ch = node_feats.shape
    slots = edge_src.shape[1]
    feat = so2_weight.shape[0]
    devices = size * reps
    group_rows = feat // devices if feat % (devices * 8) == 0 and devices & (devices - 1) == 0 else None
    feats = jnp.transpose(node_feats[0], (1, 0, 2))
    cot = jnp.transpose(out_cotangent[0], (1, 0, 2))
    charge2 = charge.reshape(1, 1)
    near = pl.pallas_call(
        functools.partial(halo_kernel, size),
        out_shape=jax.ShapeDtypeStruct((coef, NEAR * atoms, ch), BF16),
        in_specs=vmem(5),
        out_specs=vmem(1)[0],
        scratch_shapes=[
            pltpu.VMEM((coef, atoms, ch), BF16),
            pltpu.SemaphoreType.DMA((len(OFFSETS),)),
            pltpu.SemaphoreType.DMA((len(OFFSETS),)),
        ],
        compiler_params=pltpu.CompilerParams(collective_id=0, has_side_effects=True, vmem_limit_bytes=32 * MIB),
    )(feats, species.reshape(atoms, 1), charge2, species_table, charge_table)

    pos = jnp.stack([lax.axis_index("graph").astype(jnp.int32), edge_count[0, 0], jnp.int32(size)])
    if group_rows is None:
        wp_shape = jax.ShapeDtypeStruct((feat, feat), F32)
        extra = []
    else:
        wp_shape = jax.ShapeDtypeStruct((devices, 2 * group_rows, feat // 2), BF16)
        extra = [pltpu.VMEM((feat, feat), F32)]
    upd, terms, wp = pl.pallas_call(
        functools.partial(compute_kernel, group_rows),
        out_shape=(
            jax.ShapeDtypeStruct((coef, atoms, ch), BF16),
            jax.ShapeDtypeStruct((coef, NEAR * atoms, ch), BF16),
            wp_shape,
        ),
        in_specs=[pl.BlockSpec(memory_space=pltpu.SMEM)] + vmem(7),
        out_specs=tuple(vmem(3)),
        scratch_shapes=[
            pltpu.VMEM((coef, NEAR * atoms, slots), BF16),
            pltpu.VMEM((coef, atoms, slots), BF16),
            pltpu.VMEM((slots, feat), BF16),
            pltpu.VMEM((feat, slots), BF16),
            pltpu.VMEM((slots, feat), F32),
            pltpu.VMEM((slots, feat), F32),
            pltpu.VMEM((slots, feat), BF16),
        ]
        + extra,
        compiler_params=pltpu.CompilerParams(vmem_limit_bytes=56 * MIB),
    )(pos, near, feats, cot, edge_frame[0].astype(F32), edge_src, edge_dst, so2_weight)

    if group_rows is None:
        return fallback(size, upd, terms, wp, cot, species, charge)
    bits = devices.bit_length() - 1
    feat_k, wg, emb = pl.pallas_call(
        functools.partial(reduce_kernel, size, reps, bits),
        out_shape=(
            jax.ShapeDtypeStruct((coef, atoms, ch), BF16),
            jax.ShapeDtypeStruct((feat * feat // devices // 128, 128), F32),
            jax.ShapeDtypeStruct((HOTS, ch), F32),
        ),
        in_specs=vmem(5),
        out_specs=tuple(vmem(3)),
        scratch_shapes=[
            pltpu.VMEM((devices // 2 - 1, 2 * group_rows, feat // 2), BF16),
            pltpu.VMEM((devices - 1, 2 * group_rows, feat // 2), BF16),
            pltpu.VMEM((len(OFFSETS), coef, atoms, ch), BF16),
            pltpu.VMEM((bits, HOTS, ch), F32),
            pltpu.VMEM((bits, HOTS, ch), F32),
            pltpu.SemaphoreType.DMA((devices - 1,)),
            pltpu.SemaphoreType.DMA((devices - 1,)),
            pltpu.SemaphoreType.DMA((len(OFFSETS),)),
            pltpu.SemaphoreType.DMA((len(OFFSETS),)),
            pltpu.SemaphoreType.DMA((bits,)),
            pltpu.SemaphoreType.DMA((bits,)),
        ],
        compiler_params=pltpu.CompilerParams(collective_id=1, has_side_effects=True, vmem_limit_bytes=48 * MIB),
    )(terms, cot, wp, species, charge2)
    return (
        jnp.transpose(upd, (1, 0, 2))[None],
        jnp.transpose(feat_k, (1, 0, 2))[None],
        wg.reshape(-1),
        emb[:SPECIES],
        emb[SPECIES : SPECIES + CHARGES],
    )


def fallback(size, upd, terms, wp, cot, species, charge):
    atoms = cot.shape[1]
    grad = jnp.zeros(cot.shape, F32)
    for off in range(-REACH, REACH + 1):
        piece = terms[:, (off + REACH) * atoms : (off + REACH + 1) * atoms, :]
        if off:
            piece = lax.ppermute(piece, "graph", [(i, (i + off) % size) for i in range(size)])
        grad = grad + piece.astype(F32)
    feat_k = (cot.astype(F32) + grad).astype(BF16)
    ids = jnp.arange(SPECIES + CHARGES, dtype=jnp.int32)[:, None]
    hot = ((ids == species) | (ids == SPECIES + charge[None, :])).astype(F32)
    emb = lax.psum(jnp.dot(hot, grad[0], precision=PRECISE), ("graph", "rep"))
    wg = lax.psum_scatter(wp.reshape(-1), ("graph", "rep"), scatter_dimension=0, tiled=True)
    return (
        jnp.transpose(upd, (1, 0, 2))[None],
        jnp.transpose(feat_k, (1, 0, 2))[None],
        wg,
        emb[:SPECIES],
        emb[SPECIES:],
    )


def solution(mesh):
    in_specs = (
        P("rep", "graph", None, None),
        P("rep", "graph"),
        P("rep"),
        P(),
        P(),
        P(),
        P("rep", None, "graph"),
        P("rep", "graph"),
        P("rep", "graph"),
        P("rep", "graph"),
        P("rep", "graph", None, None),
    )
    out_specs = (
        P("rep", "graph", None, None),
        P("rep", "graph", None, None),
        P(("graph", "rep")),
        P(),
        P(),
    )
    body = functools.partial(local, mesh.shape["graph"], mesh.shape["rep"])
    return jax.shard_map(body, mesh=mesh, in_specs=in_specs, out_specs=out_specs, check_vma=False)
```

```python
import functools

import jax
import jax.numpy as jnp
from jax import lax
from jax.experimental import pallas as pl
from jax.experimental.pallas import tpu as pltpu
from jax.sharding import PartitionSpec as P

LMAX = 6
SPECIES = 90
CHARGES = 9
REACH = 2
NEAR = 2 * REACH + 1
MSG_SCALE = 0.25
PRECISE = lax.Precision.HIGHEST
MESH = pl.DeviceIdType.MESH
HOTS = 104
F32 = jnp.float32
BF16 = jnp.bfloat16
MIB = 1 << 20

OFFSETS = (-2, 2, -1, 1)


def degree_spans():
    return [(degree * degree, (degree + 1) * (degree + 1)) for degree in range(LMAX + 1)]


def dot_tn(left, right):
    return lax.dot_general(left, right, (((0,), (0,)), ((), ())), preferred_element_type=F32)


def dot_nn(left, right):
    return jnp.dot(left, right, preferred_element_type=F32)


def dot_nt(left, right):
    return lax.dot_general(left, right, (((1,), (1,)), ((), ())), preferred_element_type=F32)


def halo_kernel(size, feats_ref, spec_ref, charge_ref, stab_ref, ctab_ref, near_ref, hid, send_sem, recv_sem):
    atoms = feats_ref.shape[1]
    me = lax.axis_index("graph")
    rep = lax.axis_index("rep")
    odd = lax.rem(me, 2)
    across = me + 1 - 2 * odd
    above, below = lax.rem(me + 2, size), lax.rem(me + size - 2, size)
    barrier = pltpu.get_barrier_semaphore()
    for other in (above, below, across):
        pl.semaphore_signal(barrier, inc=1, device_id=(other, rep), device_id_type=MESH)
    spec_hot = (spec_ref[...] == lax.broadcasted_iota(jnp.int32, (atoms, SPECIES), 1)).astype(F32)
    charge_hot = (charge_ref[...] == lax.broadcasted_iota(jnp.int32, (atoms, CHARGES), 1)).astype(F32)
    embedding = jnp.dot(spec_hot, stab_ref[...], precision=PRECISE, preferred_element_type=F32) + jnp.dot(
        charge_hot, ctab_ref[...], precision=PRECISE, preferred_element_type=F32
    )
    hid[...] = feats_ref[...]
    hid[0] = (feats_ref[0].astype(F32) + embedding).astype(BF16)
    pl.semaphore_wait(barrier, 3)
    chunks = send_sem.shape[1]
    span = hid.shape[0] // chunks

    def place(c, slot):
        return near_ref.at[pl.ds(c * span, span), pl.ds(pl.multiple_of(slot * atoms, atoms), atoms), :]

    def move(c, source, slot, kind, other):
        return pltpu.make_async_remote_copy(
            src_ref=source,
            dst_ref=place(c, slot),
            send_sem=send_sem.at[kind, c],
            recv_sem=recv_sem.at[kind, c],
            device_id=(other, rep),
            device_id_type=MESH,
        )

    copies = []
    for c in range(chunks):
        own = hid.at[pl.ds(c * span, span)]
        copies.append(
            [
                move(c, own, 2 * REACH, 0, below),
                move(c, own, 0, 1, above),
                move(c, own, 1 + 2 * odd, 2, across),
            ]
        )
        for copy in copies[c]:
            copy.start()
    near_ref[:, pl.ds(REACH * atoms, atoms), :] = hid[...]
    far = 2 * REACH * (1 - odd)
    relays = []
    for c in range(chunks):
        arrived = pltpu.make_async_remote_copy(
            src_ref=hid.at[pl.ds(c * span, span)],
            dst_ref=place(c, far),
            send_sem=send_sem.at[0, c],
            recv_sem=recv_sem.at[odd, c],
            device_id=(across, rep),
            device_id_type=MESH,
        )
        arrived.wait_recv()
        relay = move(c, place(c, far), 3 - 2 * odd, 3, across)
        relay.start()
        relays.append(relay)
    for c in range(chunks):
        other_way = pltpu.make_async_remote_copy(
            src_ref=hid.at[pl.ds(c * span, span)],
            dst_ref=place(c, 2 * REACH - far),
            send_sem=send_sem.at[0, c],
            recv_sem=recv_sem.at[1 - odd, c],
            device_id=(across, rep),
            device_id_type=MESH,
        )
        other_way.wait_recv()
        copies[c][2].wait_recv()
        relays[c].wait_recv()
        for copy in copies[c] + [relays[c]]:
            copy.wait_send()


def compute_kernel(
    group_rows, pos_ref, near_ref, feats_ref, cot_ref, frame_ref, src_ref, dst_ref, w_ref,
    upd_ref, terms_ref, wp_ref, s_ref, d_ref, rot_ref, rott_ref, pre_ref, gv_ref, gp_ref, *rest,
):
    coef, near_atoms, ch = near_ref.shape
    atoms = feats_ref.shape[1]
    slots = src_ref.shape[1]
    me = pos_ref[0]
    live_count = pos_ref[1]
    size = pos_ref[2]
    live = lax.broadcasted_iota(jnp.int32, (1, slots), 1) < live_count
    sources = src_ref[...]
    rel = lax.rem(sources // atoms - me + REACH + size, size)
    local_src = jnp.where(live, rel * atoms + lax.rem(sources, atoms), -1)
    local_dst = jnp.where(live, dst_ref[...] - me * atoms, -1)
    s_hot = (lax.broadcasted_iota(jnp.int32, (near_atoms, slots), 0) == local_src).astype(F32)
    d_hot = (lax.broadcasted_iota(jnp.int32, (atoms, slots), 0) == local_dst).astype(F32)
    spans = degree_spans()
    for k in range(coef):
        row = frame_ref[pl.ds(k, 1), :]
        s_ref[k] = (s_hot * row).astype(BF16)
        d_ref[k] = (d_hot * row).astype(BF16)
    for l, (lo, hi) in enumerate(spans):
        cols = pl.ds(l * ch, ch)
        s_l = s_ref[lo:hi].reshape((hi - lo) * near_atoms, slots)
        rot = dot_tn(s_l, near_ref[lo:hi].reshape((hi - lo) * near_atoms, ch))
        rot_ref[:, cols] = rot.astype(BF16)
        rott_ref[cols, :] = jnp.transpose(rot).astype(BF16)
        d_l = d_ref[lo:hi].reshape((hi - lo) * atoms, slots)
        gv_ref[:, cols] = MSG_SCALE * dot_tn(d_l, cot_ref[lo:hi].reshape((hi - lo) * atoms, ch))

    def pre_body(l, carry):
        cols = pl.ds(pl.multiple_of(l * ch, ch), ch)
        pre_ref[:, cols] = dot_nn(rot_ref[...], w_ref[:, cols])
        return carry

    lax.fori_loop(0, LMAX + 1, pre_body, 0)
    sig = jax.nn.sigmoid(pre_ref[:, 0:ch])
    cross = jnp.zeros_like(sig)
    for l, (lo, hi) in enumerate(spans):
        cols = pl.ds(l * ch, ch)
        pre = pre_ref[:, cols]
        grad = gv_ref[:, cols]
        cross = cross + grad * pre
        values = (pre * sig).astype(BF16)
        d_l = d_ref[lo:hi].reshape((hi - lo) * atoms, slots)
        agg = dot_nn(d_l, values).reshape(hi - lo, atoms, ch)
        upd_ref[lo:hi] = (feats_ref[lo:hi].astype(F32) + MSG_SCALE * agg).astype(BF16)
        if l > 0:
            gp_ref[:, cols] = (grad * sig).astype(BF16)
    gp_ref[:, 0:ch] = (gv_ref[:, 0:ch] * sig + cross * sig * (1.0 - sig)).astype(BF16)

    for l, (lo, hi) in enumerate(spans):
        grad_rot = dot_nt(gp_ref[...], w_ref[pl.ds(l * ch, ch), :]).astype(BF16)
        s_l = s_ref[lo:hi].reshape((hi - lo) * near_atoms, slots)
        terms_ref[lo:hi] = dot_nn(s_l, grad_rot).astype(BF16).reshape(hi - lo, near_atoms, ch)

    if group_rows is None:

        def weight_flat(j, carry):
            cols = pl.ds(pl.multiple_of(j * ch, ch), ch)
            wp_ref[:, cols] = dot_nn(rott_ref[...], gp_ref[:, cols])
            return carry

        lax.fori_loop(0, LMAX + 1, weight_flat, 0)
        return
    wide_ref = rest[0]

    def weight_body(j, carry):
        cols = pl.ds(pl.multiple_of(j * ch, ch), ch)
        wide_ref[:, cols] = dot_nn(rott_ref[...], gp_ref[:, cols])
        return carry

    lax.fori_loop(0, LMAX + 1, weight_body, 0)
    half = wide_ref.shape[1] // 2

    def group_body(i, carry):
        rows = wide_ref[pl.ds(pl.multiple_of(i * group_rows, 8), group_rows), :]
        wp_ref[i] = jnp.concatenate([rows[:, :half], rows[:, half:]], axis=0).astype(BF16)
        return carry

    lax.fori_loop(0, wp_ref.shape[0], group_body, 0)


def bit_reversed(value, bits):
    return int(format(value, "0" + str(bits) + "b")[::-1], 2) if bits else 0


def stage_order(bits):
    return sorted(range(1 << bits), key=lambda t: -bit_reversed(t, bits))


def reduce_kernel(
    size, reps, bits, terms_ref, cot_ref, wp_ref, spec_ref, charge_ref,
    feat_ref, wg_ref, emb_ref,
    sent, got, near_got, emb_sent, emb_got, s_sem, r_sem, hs_sem, hr_sem, es_sem, er_sem,
):
    atoms = cot_ref.shape[1]
    me = lax.axis_index("graph")
    rep = lax.axis_index("rep")
    mine = me * reps + rep
    bit = [lax.rem(mine // (1 << b), 2) for b in range(bits)]

    def flipped(rel):
        total = 0
        for b in range(bits):
            total = total + (1 << b) * ((1 - bit[b]) if (rel >> b) & 1 else bit[b])
        return total

    def partner(b):
        other = flipped(1 << b)
        return (other // reps, lax.rem(other, reps))

    near_ids = [(lax.rem(me + off + size, size), rep) for off in OFFSETS]
    barrier = pltpu.get_barrier_semaphore()
    for device in near_ids + [partner(b) for b in range(bits)]:
        pl.semaphore_signal(barrier, inc=1, device_id=device, device_id_type=MESH)
    pl.semaphore_wait(barrier, len(near_ids) + bits)

    halo = []
    for i, off in enumerate(OFFSETS):
        copy = pltpu.make_async_remote_copy(
            src_ref=terms_ref.at[:, pl.ds((off + REACH) * atoms, atoms), :],
            dst_ref=near_got.at[i],
            send_sem=hs_sem.at[i],
            recv_sem=hr_sem.at[i],
            device_id=near_ids[i],
            device_id_type=MESH,
        )
        halo.append(copy)
    base = [sum(1 << (bits - 1 - q) for q in range(stage)) for stage in range(bits + 1)]
    copies = {}

    def launch(stage, t, source):
        slot = base[stage] + t
        copy = pltpu.make_async_remote_copy(
            src_ref=source,
            dst_ref=got.at[slot],
            send_sem=s_sem.at[slot],
            recv_sem=r_sem.at[slot],
            device_id=partner(stage),
            device_id_type=MESH,
        )
        copy.start()
        copies[stage, t] = copy

    for t in stage_order(bits - 1):
        launch(0, t, wp_ref.at[flipped(2 * t + 1)])
    for copy in halo:
        copy.start()

    def summed(stage, rel):
        total = wp_ref[flipped(rel)].astype(F32)
        for q in range(stage):
            total = total + got[base[q] + (rel >> (q + 1))].astype(F32)
        return total

    def advance(stage):
        for t in stage_order(bits - 1 - stage):
            rel = (2 * t + 1) << stage
            slot = base[stage] + t
            for q in range(stage):
                copies[q, rel >> (q + 1)].wait_recv()
            sent[slot - base[1]] = summed(stage, rel).astype(BF16)
            launch(stage, t, sent.at[slot - base[1]])

    emb = []

    def emb_send(b):
        emb_sent[b] = emb_ref[...]
        copy = pltpu.make_async_remote_copy(
            src_ref=emb_sent.at[b],
            dst_ref=emb_got.at[b],
            send_sem=es_sem.at[b],
            recv_sem=er_sem.at[b],
            device_id=partner(b),
            device_id_type=MESH,
        )
        copy.start()
        emb.append(copy)

    def emb_take(b):
        emb[b].wait_recv()
        emb_ref[...] = emb_ref[...] + emb_got[b]

    def finish_nodes():
        for copy in halo:
            copy.wait_recv()
        grad = terms_ref[:, pl.ds(REACH * atoms, atoms), :].astype(F32)
        for i in range(len(OFFSETS)):
            grad = grad + near_got[i].astype(F32)
        feat_ref[...] = (cot_ref[...].astype(F32) + grad).astype(BF16)
        row_ids = lax.broadcasted_iota(jnp.int32, (HOTS, atoms), 0)
        hot = ((row_ids == spec_ref[...]) | (row_ids == SPECIES + charge_ref[...])).astype(F32)
        emb_ref[...] = jnp.dot(hot, grad[0], precision=PRECISE, preferred_element_type=F32)

    advance(1)
    advance(2)
    finish_nodes()
    emb_send(0)
    taken = 0
    for stage in range(3, bits):
        advance(stage)
        emb_take(taken)
        taken += 1
        emb_send(taken)
    while taken < bits:
        emb_take(taken)
        taken += 1
        if taken < bits:
            emb_send(taken)

    for q in range(bits):
        copies[q, 0].wait_recv()
    total = summed(bits, 0)
    rows = wg_ref.shape[0] // 14
    for j in range(14):
        lanes = (j % 7) * 128
        part = (j // 7) * rows
        wg_ref[pl.ds(j, rows, stride=14), :] = total[part : part + rows, lanes : lanes + 128]
    for copy in list(copies.values()) + halo + emb:
        copy.wait_send()


def vmem(count):
    return [pl.BlockSpec(memory_space=pltpu.VMEM)] * count


def local(
    size, reps, node_feats, species, charge, species_table, charge_table, so2_weight,
    edge_frame, edge_src, edge_dst, edge_count, out_cotangent,
):
    _, atoms, coef, ch = node_feats.shape
    slots = edge_src.shape[1]
    feat = so2_weight.shape[0]
    devices = size * reps
    group_rows = feat // devices if feat % (devices * 8) == 0 and devices & (devices - 1) == 0 else None
    feats = jnp.transpose(node_feats[0], (1, 0, 2))
    cot = jnp.transpose(out_cotangent[0], (1, 0, 2))
    charge2 = charge.reshape(1, 1)
    chunks = LMAX + 1 if coef % (LMAX + 1) == 0 else 1
    near = pl.pallas_call(
        functools.partial(halo_kernel, size),
        out_shape=jax.ShapeDtypeStruct((coef, NEAR * atoms, ch), BF16),
        in_specs=vmem(5),
        out_specs=vmem(1)[0],
        scratch_shapes=[
            pltpu.VMEM((coef, atoms, ch), BF16),
            pltpu.SemaphoreType.DMA((4, chunks)),
            pltpu.SemaphoreType.DMA((4, chunks)),
        ],
        compiler_params=pltpu.CompilerParams(collective_id=0, has_side_effects=True, vmem_limit_bytes=32 * MIB),
    )(feats, species.reshape(atoms, 1), charge2, species_table, charge_table)

    pos = jnp.stack([lax.axis_index("graph").astype(jnp.int32), edge_count[0, 0], jnp.int32(size)])
    if group_rows is None:
        wp_shape = jax.ShapeDtypeStruct((feat, feat), F32)
        extra = []
    else:
        wp_shape = jax.ShapeDtypeStruct((devices, 2 * group_rows, feat // 2), BF16)
        extra = [pltpu.VMEM((feat, feat), F32)]
    upd, terms, wp = pl.pallas_call(
        functools.partial(compute_kernel, group_rows),
        out_shape=(
            jax.ShapeDtypeStruct((coef, atoms, ch), BF16),
            jax.ShapeDtypeStruct((coef, NEAR * atoms, ch), BF16),
            wp_shape,
        ),
        in_specs=[pl.BlockSpec(memory_space=pltpu.SMEM)] + vmem(7),
        out_specs=tuple(vmem(3)),
        scratch_shapes=[
            pltpu.VMEM((coef, NEAR * atoms, slots), BF16),
            pltpu.VMEM((coef, atoms, slots), BF16),
            pltpu.VMEM((slots, feat), BF16),
            pltpu.VMEM((feat, slots), BF16),
            pltpu.VMEM((slots, feat), F32),
            pltpu.VMEM((slots, feat), F32),
            pltpu.VMEM((slots, feat), BF16),
        ]
        + extra,
        compiler_params=pltpu.CompilerParams(vmem_limit_bytes=56 * MIB),
    )(pos, near, feats, cot, edge_frame[0].astype(F32), edge_src, edge_dst, so2_weight)

    if group_rows is None:
        return fallback(size, upd, terms, wp, cot, species, charge)
    bits = devices.bit_length() - 1
    feat_k, wg, emb = pl.pallas_call(
        functools.partial(reduce_kernel, size, reps, bits),
        out_shape=(
            jax.ShapeDtypeStruct((coef, atoms, ch), BF16),
            jax.ShapeDtypeStruct((feat * feat // devices // 128, 128), F32),
            jax.ShapeDtypeStruct((HOTS, ch), F32),
        ),
        in_specs=vmem(5),
        out_specs=tuple(vmem(3)),
        scratch_shapes=[
            pltpu.VMEM((devices // 2 - 1, 2 * group_rows, feat // 2), BF16),
            pltpu.VMEM((devices - 1, 2 * group_rows, feat // 2), BF16),
            pltpu.VMEM((len(OFFSETS), coef, atoms, ch), BF16),
            pltpu.VMEM((bits, HOTS, ch), F32),
            pltpu.VMEM((bits, HOTS, ch), F32),
            pltpu.SemaphoreType.DMA((devices - 1,)),
            pltpu.SemaphoreType.DMA((devices - 1,)),
            pltpu.SemaphoreType.DMA((len(OFFSETS),)),
            pltpu.SemaphoreType.DMA((len(OFFSETS),)),
            pltpu.SemaphoreType.DMA((bits,)),
            pltpu.SemaphoreType.DMA((bits,)),
        ],
        compiler_params=pltpu.CompilerParams(collective_id=1, has_side_effects=True, vmem_limit_bytes=48 * MIB),
    )(terms, cot, wp, species, charge2)
    return (
        jnp.transpose(upd, (1, 0, 2))[None],
        jnp.transpose(feat_k, (1, 0, 2))[None],
        wg.reshape(-1),
        emb[:SPECIES],
        emb[SPECIES : SPECIES + CHARGES],
    )


def fallback(size, upd, terms, wp, cot, species, charge):
    atoms = cot.shape[1]
    grad = jnp.zeros(cot.shape, F32)
    for off in range(-REACH, REACH + 1):
        piece = terms[:, (off + REACH) * atoms : (off + REACH + 1) * atoms, :]
        if off:
            piece = lax.ppermute(piece, "graph", [(i, (i + off) % size) for i in range(size)])
        grad = grad + piece.astype(F32)
    feat_k = (cot.astype(F32) + grad).astype(BF16)
    ids = jnp.arange(SPECIES + CHARGES, dtype=jnp.int32)[:, None]
    hot = ((ids == species) | (ids == SPECIES + charge[None, :])).astype(F32)
    emb = lax.psum(jnp.dot(hot, grad[0], precision=PRECISE), ("graph", "rep"))
    wg = lax.psum_scatter(wp.reshape(-1), ("graph", "rep"), scatter_dimension=0, tiled=True)
    return (
        jnp.transpose(upd, (1, 0, 2))[None],
        jnp.transpose(feat_k, (1, 0, 2))[None],
        wg,
        emb[:SPECIES],
        emb[SPECIES:],
    )


def solution(mesh):
    in_specs = (
        P("rep", "graph", None, None),
        P("rep", "graph"),
        P("rep"),
        P(),
        P(),
        P(),
        P("rep", None, "graph"),
        P("rep", "graph"),
        P("rep", "graph"),
        P("rep", "graph"),
        P("rep", "graph", None, None),
    )
    out_specs = (
        P("rep", "graph", None, None),
        P("rep", "graph", None, None),
        P(("graph", "rep")),
        P(),
        P(),
    )
    body = functools.partial(local, mesh.shape["graph"], mesh.shape["rep"])
    return jax.shard_map(body, mesh=mesh, in_specs=in_specs, out_specs=out_specs, check_vma=False)
```
